32 devices in a mesh: mode: 4 (over z), ty: 4 (over y, core), tx: 2 (over x).
Axes of the slice: x: 2, y: 2, z: 4, core: 2. Of those that a mesh axis runs over, the one named last changes fastest.
Arguments:
- object_slices: float32 [4, 2, 512, 256], P(None, None, 'ty', 'tx'), may hold values from -4.2 to 4.2
- probe_modes: float32 [16, 2, 128, 128], P('mode'), may hold values from -1.5 to 1.5
- positions: int32 [4, 2, 1, 2], P('ty', 'tx'), may hold values from 0 to 128
- measured: float32 [4, 2, 1, 128, 128], P('ty', 'tx'), may hold values from 0.3 to 3
Outputs:
- object_gradient: float32 [4, 2, 512, 256], P('mode', None, 'ty', 'tx')
The draws below stay inside these ranges and needn't reach their ends.
Inputs may be any that keep to these rules, and one draw needn't show every extreme that they name: `positions`: pattern k of tile (a, b) has its 128 x 128 window inside that tile's region, which reaches 64 pixels beyond the tile on every side.
All inputs are finite; a program needn't handle non-finite values.
Results may differ from the reference program's by a relative error of at most 0.00016.
Values sent between devices are 32-bit elements; how exact they have to be, the bound alone decides.
No kernel may reach another device: no remote copies, remote signals or barrier semaphores. Data moves between devices by JAX's collectives and lax.ppermute only.
A program may use at most 64 MiB of HBM per device.

```python
import math
import jax
import jax.numpy as jnp
from jax import lax

DET = 128
MODES = 16
SLICES = 4
TILE = 128
MARGIN = 64
PAT_DEV = 1
EXT = 256
TILES_Y = 4
TILES_X = 2
NY = 512
NX = 256


def place_ends(drawn, rng, least, high):
    longest = drawn.shape.index(max(drawn.shape))
    spots = []
    for shift in (0, 1):
        where = [jax.random.randint(jax.random.fold_in(rng, axis), (), 0, length) for axis, length in enumerate(drawn.shape)]
        where[longest] = (where[longest] + shift) % drawn.shape[longest]
        spots.append(tuple(where))
    return drawn.at[spots[0]].set(least).at[spots[1]].set(high)


def levels(own_key, shape, pieces, smallest, high):
    level, own = 1.0, jax.random.fold_in(own_key, 6)
    for dim, parts in pieces:
        heights = jnp.exp(jax.random.uniform(jax.random.fold_in(own, dim), (parts,), jnp.float32, smallest / len(pieces), high / len(pieces)))
        level = level * jnp.repeat(heights, shape[dim] // parts).reshape([-1 if axis == dim else 1 for axis in range(len(shape))])
    return level


def noise(rng, extent, spread, reach, pieces=(), kind=jnp.bfloat16):
    gain = levels(rng, extent, pieces, -0.22, 0.18) if pieces else 1.0
    entries = jax.random.normal(rng, extent, jnp.float32) * spread * gain
    return jnp.minimum(jnp.maximum(entries, -reach), reach).astype(kind)


def setup_inputs(seed: int = 0) -> dict:
    key_of = jax.random.split(jax.random.key(seed), 5)
    return {
        "object_slices": noise(key_of[0], (SLICES, 2, NY, NX), 0.7, 4.2, ((2, 4), (3, 2)), jnp.float32),
        "probe_modes": noise(key_of[1], (MODES, 2, DET, DET), 0.25, 1.5, ((0, 4),), jnp.float32),
        "positions": place_ends(jax.random.randint(key_of[2], (TILES_Y, TILES_X, PAT_DEV, 2), 0, EXT - DET + 1), jax.random.fold_in(key_of[2], 1), 0, EXT - DET).astype(jnp.int32),
        "measured": jnp.clip(jnp.exp(math.log(3.0) - 2.3025851 * jax.random.uniform(key_of[3], (TILES_Y, TILES_X, PAT_DEV, DET, DET), jnp.float32) ** levels(key_of[3], (TILES_Y, TILES_X, PAT_DEV, DET, DET), ((0, 4), (1, 2)), -0.2, 0.2)), 0.3, 3.0),
    }


fresnel_rate = 0.3

def chirp_phase(length, kind):
    counter = jnp.arange(length)
    frequency = jnp.where(counter < length // 2, counter, counter - length).astype(kind)
    return fresnel_rate * (frequency[:, None] ** 2 + frequency[None, :] ** 2) / length

def forward_fourier(field):
    return jnp.fft.fft2(field, norm='ortho')

def inverse_fourier(field):
    return jnp.fft.ifft2(field, norm='ortho')

def reference(object_slices, probe_modes, positions, measured):
    transmission = lax.complex(object_slices[:, 0], object_slices[:, 1])
    transmission = jnp.pad(transmission, ((0, 0), (MARGIN, MARGIN), (MARGIN, MARGIN)))
    illumination = lax.complex(probe_modes[:, 0], probe_modes[:, 1])
    phase = chirp_phase(DET, jnp.float32)
    kernel = lax.complex(jnp.cos(phase), -jnp.sin(phase))
    row_start = (positions[..., 0] + TILE * jnp.arange(TILES_Y, dtype=jnp.int32)[:, None, None]).reshape(-1).astype(jnp.int32)
    col_start = (positions[..., 1] + TILE * jnp.arange(TILES_X, dtype=jnp.int32)[None, :, None]).reshape(-1).astype(jnp.int32)
    amplitudes = measured.reshape(-1, DET, DET)

    def accumulate(summed, item):
        row, column, amplitude = item
        anchor = (jnp.int32(0), row, column)
        window = lax.dynamic_slice(transmission, anchor, (SLICES, DET, DET))
        wavefield = illumination
        incident = []
        farfield = wavefield
        for layer_index in range(SLICES):
            incident.append(wavefield)
            leaving = wavefield * window[layer_index]
            if layer_index + 1 < SLICES:
                wavefield = inverse_fourier(kernel * forward_fourier(leaving))
            else:
                farfield = forward_fourier(leaving)
        intensity = lax.optimization_barrier(jnp.sum(jnp.real(farfield) ** 2 + jnp.imag(farfield) ** 2, axis=0))
        weight = 1.0 - amplitude / jnp.maximum(jnp.sqrt(intensity), 1.0)
        backward = inverse_fourier(weight * farfield)
        gradients = [None] * SLICES
        for layer_index in reversed(range(SLICES)):
            gradients[layer_index] = lax.optimization_barrier(jnp.sum(jnp.conj(incident[layer_index]) * backward, axis=0))
            if layer_index > 0:
                backward = inverse_fourier(jnp.conj(kernel) * forward_fourier(jnp.conj(window[layer_index]) * backward))
        update = jnp.stack(gradients)
        current = lax.dynamic_slice(summed, anchor, (SLICES, DET, DET))
        return (lax.dynamic_update_slice(summed, current + update, anchor), None)
    summed, ignored = lax.scan(accumulate, jnp.zeros_like(transmission), (row_start, col_start, amplitudes))
    inner = summed[:, MARGIN:MARGIN + NY, MARGIN:MARGIN + NX]
    return jnp.stack([jnp.real(inner), jnp.imag(inner)], axis=1)
```

```python
import functools

import jax
import jax.numpy as jnp
import numpy as np
from jax import lax
from jax.experimental import pallas as pl
from jax.experimental.pallas import tpu as pltpu
from jax.sharding import PartitionSpec as P

FRESNEL_RATE = 0.3
F32, BF16 = jnp.float32, jnp.bfloat16
VMEM_LIMIT = 40 * 2**20


def pair(high, low):
    first = high.astype(jnp.bfloat16)
    return [first, (low - first.astype(np.float64)).astype(jnp.bfloat16)]


def tables(length):
    counter = np.arange(length)
    fourier = np.exp(-2j * np.pi / length * (np.outer(counter, counter) % length)) / np.sqrt(length)
    frequency = np.where(counter < length // 2, counter, counter - length).astype(np.float64)
    chirp = np.exp(-1j * FRESNEL_RATE * frequency**2 / length)
    moved = fourier.conj() @ (chirp[:, None] * fourier)
    stacked = []
    for matrix in (moved, fourier):
        right = np.block([[matrix.real, matrix.imag], [-matrix.imag, matrix.real]])
        stacked += pair(right, right) + pair(right.T, right.T)
    return np.stack(stacked)


def dot(left, right):
    return jnp.dot(left, right, preferred_element_type=F32)


def split(value):
    high = value.astype(BF16)
    return high, (value - high.astype(F32)).astype(BF16)


def two_sided(planes, table_ref, base, conjugate):
    det = planes[0][0].shape[0]
    right, left = (base + 2, base) if conjugate else (base, base + 2)
    field = jnp.concatenate([jnp.concatenate(mode, 1) for mode in planes], 0)
    high, low = split(field)
    upper = dot(high, table_ref[right]) + dot(low, table_ref[right]) + dot(high, table_ref[right + 1])
    columns = []
    for part in split(upper):
        first, second = part[:det], part[det:]
        real = jnp.concatenate([first[:, :det], second[:, :det]], 1)
        imag = jnp.concatenate([first[:, det:], second[:, det:]], 1)
        columns.append(jnp.concatenate([real, imag], 0))
    high, low = columns
    both = dot(table_ref[left], high) + dot(table_ref[left], low) + dot(table_ref[left + 1], high)
    return [(both[:det, j * det : (j + 1) * det], both[det:, j * det : (j + 1) * det]) for j in range(2)]


def iota(shape, dim):
    return lax.broadcasted_iota(jnp.int32, shape, dim)


def half_roll(plane):
    return pltpu.roll(plane, plane.shape[1] // 2, 1)


def is_right(index, parity):
    return lax.rem(index, 2) == parity


def window_rows(above, tile, below, start):
    det = tile.shape[0]
    half = det // 2
    first = jnp.concatenate([above, tile[:half]], 0)
    second = jnp.concatenate([tile[half:], below], 0)
    mixed = jnp.where(iota(first.shape, 0) >= start, first, second)
    return pltpu.roll(mixed, lax.rem(det - start, det), 0)


def pack_kernel(parities, column_axis, tile_ref, above_ref, below_ref, *refs):
    count = len(parities)
    place_refs, message_refs = refs[:count], refs[count:]
    column = lax.axis_index(column_axis)
    for parity, place_ref, message_ref in zip(parities, place_refs, message_refs):
        start = place_ref[0]
        right = is_right(column, parity)
        for s in range(tile_ref.shape[0]):
            real, imag = [window_rows(above_ref[s, c], tile_ref[s, c], below_ref[s, c], start) for c in range(2)]
            lower = iota(real.shape, 1) < real.shape[1] // 2
            to_right = jnp.where(lower, half_roll(real), imag)
            to_left = jnp.where(lower, real, half_roll(imag))
            message_ref[s] = jnp.where(right, to_right, to_left)


def forward_kernel(parities, column_axis, place_ref, tile_ref, above_ref, below_ref, table_ref, *refs):
    count = len(parities)
    message_refs, probe_refs = refs[:count], refs[count : count + 3]
    window_ref, wave_ref, far_ref, intensity_ref = refs[count + 3 :]
    slices, _, det, _ = tile_ref.shape
    row, col = place_ref[0], place_ref[1]
    column = lax.axis_index(column_axis)
    lanes = iota((det, det), 1)
    lower = lanes < det // 2
    late = lanes >= col
    back_shift = lax.rem(det - col, det)
    probes = [(ref, j) for ref in probe_refs for j in range(ref.shape[0])]
    for s in range(slices):
        messages = [ref[s] for ref in message_refs]
        for c in range(2):
            own = half_roll(window_rows(above_ref[s, c], tile_ref[s, c], below_ref[s, c], row))
            left, right = jnp.zeros_like(own), jnp.zeros_like(own)
            for parity, message in zip(parities, messages):
                turned = half_roll(message)
                at_right = is_right(column, parity)
                right = right + jnp.where(at_right, turned if c == 0 else message, 0.0)
                left = left + jnp.where(at_right, 0.0, message if c == 0 else turned)
            early_block = jnp.where(lower, left, own)
            late_block = jnp.where(lower, own, right)
            window_ref[s, c] = pltpu.roll(jnp.where(late, early_block, late_block), back_shift, 1)
    total = jnp.zeros((det, det), F32)
    for s in range(slices):
        real, imag = window_ref[s, 0], window_ref[s, 1]
        for first in range(0, len(probes), 2):
            planes = []
            for mode in (first, first + 1):
                if s == 0:
                    ref, j = probes[mode]
                    wave_real, wave_imag = ref[j, 0], ref[j, 1]
                else:
                    wave_real, wave_imag = wave_ref[s - 1, mode, 0], wave_ref[s - 1, mode, 1]
                planes.append((wave_real * real - wave_imag * imag, wave_real * imag + wave_imag * real))
            last = s == slices - 1
            result = two_sided(planes, table_ref, 4 if last else 0, False)
            for j, (out_real, out_imag) in enumerate(result):
                target = far_ref.at[first + j] if last else wave_ref.at[s, first + j]
                target[0] = out_real
                target[1] = out_imag
                if last:
                    total = total + (out_real * out_real + out_imag * out_imag)
    intensity_ref[...] = total


def backward_kernel(parities, mode_axis, column_axis, place_ref, measured_ref, mine_ref, other_ref, table_ref, *refs):
    count = len(parities)
    probe_refs, (window_ref, wave_ref, far_ref) = refs[:3], refs[3:6]
    center_ref, send_ref = refs[6:8]
    strip_refs, send_strip_refs = refs[8 : 8 + count], refs[8 + count : 8 + 2 * count]
    keep_ref, back_ref = refs[8 + 2 * count :]
    slices, _, det, _ = window_ref.shape
    modes = far_ref.shape[0]
    col = place_ref[1]
    me = lax.axis_index(mode_axis)
    peer = me + 1 - 2 * lax.rem(me, 2)
    column = lax.axis_index(column_axis)
    probes = [(ref, j) for ref in probe_refs for j in range(ref.shape[0])]
    intensity = mine_ref[...] + other_ref[...]
    weight = 1.0 - measured_ref[...] / jnp.maximum(jnp.sqrt(intensity), 1.0)
    for s in reversed(range(slices)):
        last = s == slices - 1
        term_real, term_imag = jnp.zeros((det, det), F32), jnp.zeros((det, det), F32)
        if not last:
            real, imag = window_ref[s + 1, 0], window_ref[s + 1, 1]
        for first in range(0, modes, 2):
            planes = []
            for mode in (first, first + 1):
                if last:
                    planes.append((weight * far_ref[mode, 0], weight * far_ref[mode, 1]))
                else:
                    back_real, back_imag = back_ref[mode, 0], back_ref[mode, 1]
                    planes.append((real * back_real + imag * back_imag, real * back_imag - imag * back_real))
            result = two_sided(planes, table_ref, 4 if last else 0, True)
            for j, (back_real, back_imag) in enumerate(result):
                mode = first + j
                if s > 0:
                    back_ref[mode, 0] = back_real
                    back_ref[mode, 1] = back_imag
                    wave_real, wave_imag = wave_ref[s - 1, mode, 0], wave_ref[s - 1, mode, 1]
                else:
                    ref, k = probes[mode]
                    wave_real, wave_imag = ref[k, 0], ref[k, 1]
                term_real = term_real + (wave_real * back_real + wave_imag * back_imag)
                term_imag = term_imag + (wave_real * back_imag - wave_imag * back_real)
        for slot, owner in ((0, me), (1, peer)):

            @pl.when(owner == s)
            def _(slot=slot, term_real=term_real, term_imag=term_imag):
                keep_ref[slot, 0] = term_real
                keep_ref[slot, 1] = term_imag

    lanes = iota((det, det), 1)
    lower, late = lanes < det // 2, lanes >= col
    forth_shift = lax.rem(col, det)
    for slot, middle_ref, out_strip_refs in ((0, center_ref, strip_refs), (1, send_ref, send_strip_refs)):
        early, latter = [], []
        for c in range(2):
            turned = pltpu.roll(keep_ref[slot, c], forth_shift, 1)
            early.append(jnp.where(late, turned, 0.0))
            latter.append(jnp.where(late, 0.0, turned))
            middle_ref[c] = half_roll(jnp.where(lower, latter[c], early[c]))
        to_right = jnp.where(lower, half_roll(latter[0]), latter[1])
        to_left = jnp.where(lower, early[0], half_roll(early[1]))
        for parity, strip_ref in zip(parities, out_strip_refs):
            strip_ref[...] = jnp.where(is_right(column, parity), to_right, to_left)


def place_kernel(parities, column_axis, place_ref, mine_ref, other_ref, *refs):
    count = len(parities)
    place_refs, one_refs, two_refs = refs[:count], refs[count : 2 * count], refs[2 * count : 3 * count]
    middle_ref, up_ref, down_ref = refs[3 * count :]
    det = mine_ref.shape[1]
    half = det // 2
    column = lax.axis_index(column_axis)
    rows, lower = iota((det, det), 0), iota((det, det), 1) < half
    start = place_ref[0]

    def placed(plane, begin):
        turned = pltpu.roll(plane, lax.rem(begin, det), 0)
        late = rows >= begin
        return jnp.where(late, turned, 0.0), jnp.where(late, 0.0, turned)

    blocks = [list(placed(mine_ref[c] + other_ref[c], start)) for c in range(2)]
    for parity, partner_ref, one_ref, two_ref in zip(parities, place_refs, one_refs, two_refs):
        strip = one_ref[...] + two_ref[...]
        at_right = is_right(column, parity)
        for block, part in enumerate(placed(strip, partner_ref[0])):
            turned = half_roll(part)
            real = jnp.where(lower != at_right, jnp.where(at_right, turned, part), 0.0)
            imag = jnp.where(lower != at_right, jnp.where(at_right, part, turned), 0.0)
            blocks[0][block] = blocks[0][block] + real
            blocks[1][block] = blocks[1][block] + imag
    for c in range(2):
        first, second = blocks[c]
        up_ref[c] = first[:half]
        middle_ref[c, :half] = first[half:]
        middle_ref[c, half:] = second[:half]
        down_ref[c] = second[half:]


SMEM_SPEC = pl.BlockSpec(memory_space=pltpu.SMEM)
VMEM_SPEC = pl.BlockSpec(memory_space=pltpu.VMEM)


def call(kernel, outs, operands, scratch=(), scalars=()):
    return pl.pallas_call(
        kernel,
        out_shape=outs,
        in_specs=[SMEM_SPEC if i in scalars else VMEM_SPEC for i in range(len(operands))],
        out_specs=jax.tree.map(lambda _: VMEM_SPEC, outs),
        scratch_shapes=scratch,
        compiler_params=pltpu.CompilerParams(vmem_limit_bytes=VMEM_LIMIT),
    )(*operands)


def body(object_slices, probe_modes, positions, measured):
    modes_here, _, det, _ = probe_modes.shape
    slices, half = object_slices.shape[0], det // 2
    groups, height, width = lax.axis_size("mode"), lax.axis_size("ty"), lax.axis_size("tx")
    place = positions.reshape(2)

    upward = [(i, i - 1) for i in range(1, height)]
    downward = [(i - 1, i) for i in range(1, height)]
    parities = (0,) if width == 2 else (0, 1)

    def edges(parity):
        ends = [(i, i + 1) for i in range(parity, width - 1, 2)]
        return ends + [(j, i) for i, j in ends]

    mirror = [(i, groups - 1 - i) for i in range(groups)]
    neighbour = [(i, i ^ 1) for i in range(groups)]

    above = lax.ppermute(object_slices[:, :, half:], "ty", downward)
    below = lax.ppermute(object_slices[:, :, :half], "ty", upward)
    partner_places = [lax.ppermute(place, "tx", edges(parity)) for parity in parities]
    row_parity = lax.rem(lax.axis_index("ty"), 2)
    part = lax.dynamic_slice_in_dim(probe_modes, row_parity * (modes_here // 2), modes_here // 2, 0)
    far_half = lax.ppermute(part, "mode", mirror)
    swap = [(i, i ^ 1) for i in range(height)]
    near_half = lax.ppermute(far_half, "ty", swap)
    probes = [probe_modes, far_half, near_half]

    count = len(parities)
    message = jax.ShapeDtypeStruct((slices, det, det), F32)
    messages = call(
        functools.partial(pack_kernel, parities, "tx"),
        [message] * count,
        [object_slices, above, below, *partner_places],
        scalars=range(3, 3 + count),
    )
    messages = [lax.ppermute(block, "tx", edges(parity)) for parity, block in zip(parities, messages)]

    table = jnp.asarray(tables(det))
    modes = 2 * modes_here
    plane = jax.ShapeDtypeStruct((det, det), F32)
    complex_plane = jax.ShapeDtypeStruct((2, det, det), F32)
    window, wave, far, mine = call(
        functools.partial(forward_kernel, parities, "tx"),
        [
            jax.ShapeDtypeStruct((slices, 2, det, det), F32),
            jax.ShapeDtypeStruct((slices - 1, modes, 2, det, det), F32),
            jax.ShapeDtypeStruct((modes, 2, det, det), F32),
            plane,
        ],
        [place, object_slices, above, below, table, *messages, *probes],
        scalars=(0,),
    )
    other = lax.ppermute(mine, "mode", neighbour)
    center, send, *strips = call(
        functools.partial(backward_kernel, parities, "mode", "tx"),
        [complex_plane] * 2 + [plane] * (2 * count),
        [place, measured.reshape(det, det), mine, other, table, *probes, window, wave, far],
        scratch=[pltpu.VMEM((2, 2, det, det), F32), pltpu.VMEM((modes, 2, det, det), F32)],
        scalars=(0,),
    )
    received = lax.ppermute(send, "mode", neighbour)
    ones = [lax.ppermute(block, "tx", edges(parity)) for parity, block in zip(parities, strips[:count])]
    twos = []
    for parity, block in zip(parities, strips[count:]):
        route = [(i * width + p, j * width + q) for i, j in neighbour for p, q in edges(parity)]
        twos.append(lax.ppermute(block, ("mode", "tx"), route))
    strip = jax.ShapeDtypeStruct((2, half, det), F32)
    middle, up, down = call(
        functools.partial(place_kernel, parities, "tx"),
        [complex_plane, strip, strip],
        [place, center, received, *partner_places, *ones, *twos],
        scalars=(0, *range(3, 3 + count)),
    )
    from_below = lax.ppermute(up, "ty", upward)
    from_above = lax.ppermute(down, "ty", downward)
    return (middle + jnp.concatenate([from_above, from_below], 1))[None]


def solution(mesh):
    return jax.shard_map(
        body,
        mesh=mesh,
        in_specs=(
            P(None, None, "ty", "tx"),
            P("mode", None, None, None),
            P("ty", "tx", None, None),
            P("ty", "tx", None, None, None),
        ),
        out_specs=P("mode", None, "ty", "tx"),
        check_vma=False,
    )
```

```python
import functools

import jax
import jax.numpy as jnp
import numpy as np
from jax import lax
from jax.experimental import pallas as pl
from jax.experimental.pallas import tpu as pltpu
from jax.sharding import PartitionSpec as P

FRESNEL_RATE = 0.3
F32, BF16 = jnp.float32, jnp.bfloat16
VMEM_LIMIT = 24 * 2**20
ROWS = 32
SHARES = 2
MOVE, MOVE_BACK, FOURIER, FOURIER_BACK = 0, 2, 4, 6


def pair(table):
    high = table.astype(jnp.bfloat16)
    return [high, (table - high.astype(np.float64)).astype(jnp.bfloat16)]


def tables(length):
    counter = np.arange(length)
    fourier = np.exp(-2j * np.pi / length * (np.outer(counter, counter) % length)) / np.sqrt(length)
    frequency = np.where(counter < length // 2, counter, counter - length).astype(np.float64)
    chirp = np.exp(-1j * FRESNEL_RATE * frequency**2 / length)
    moved = fourier.conj() @ (chirp[:, None] * fourier)
    stacked = []
    for matrix in (moved, fourier):
        right = np.block([[matrix.real, matrix.imag], [-matrix.imag, matrix.real]])
        stacked += pair(right) + pair(right.T)
    return np.stack(stacked)


def dot(left, right):
    return jnp.dot(left, right, preferred_element_type=F32)


def split(value):
    high = value.astype(BF16)
    return high, (value - high.astype(F32)).astype(BF16)


def one_side(real, imag, table_ref, base):
    high, low = split(jnp.concatenate([real, imag], 1))
    both = dot(high, table_ref[base]) + dot(low, table_ref[base]) + dot(high, table_ref[base + 1])
    det = real.shape[1]
    return both[:, :det], both[:, det:]


def two_sided(real, imag, table_ref, base):
    upper_real, upper_imag = one_side(real, imag, table_ref, base)
    return one_side(upper_real.T, upper_imag.T, table_ref, base)


def iota(shape, dim):
    return lax.broadcasted_iota(jnp.int32, shape, dim)


def half_roll(plane):
    return pltpu.roll(plane, plane.shape[1] // 2, 1)


def is_right(index, parity):
    return lax.rem(index, 2) == parity


def has_partner(axis, parity):
    index = lax.axis_index(axis)
    first = index - lax.rem(index + parity, 2)
    return (first >= 0) & (first + 1 < lax.axis_size(axis))


def scalar(ref, *index):
    return jnp.max(ref[index])


def window_rows(above, tile, below, start):
    det = tile.shape[0]
    half = det // 2
    first = jnp.concatenate([above, tile[:half]], 0)
    second = jnp.concatenate([tile[half:], below], 0)
    mixed = jnp.where(iota(first.shape, 0) >= start, first, second)
    return pltpu.roll(mixed, lax.rem(det - start, det), 0)


def half_rows(ref_slice, row_parity, edge):
    half = ref_slice // 2
    return pl.multiple_of(jnp.where(row_parity == edge, half, 0), half)


def start_kernel(parities, row_axis, column_axis, place_hbm, tile_hbm, probe_hbm, *refs):
    count = len(parities)
    place_ref, tile_ref, part_ref, refs = refs[0], refs[1], refs[2], refs[3:]
    edge_refs, message_refs, place_smem, sems = refs[:2], refs[2 : 2 + count], refs[2 + count], refs[3 + count]
    slices, _, det, _ = tile_ref.shape
    share = part_ref.shape[0]
    row = lax.axis_index(row_axis)
    row_parity = lax.rem(row, 2)
    column = lax.axis_index(column_axis)
    whole = [pltpu.make_async_copy(tile_hbm.at[s], tile_ref.at[s], sems.at[s]) for s in range(slices)]
    sources = [(probe_hbm.at[pl.ds(lax.rem(row, SHARES) * share, share)], part_ref)]
    for edge, edge_ref in enumerate(edge_refs):
        first = half_rows(det, row_parity, edge)
        sources.append((tile_hbm.at[:, :, pl.ds(first, det // 2)], edge_ref))
    sources.append((place_hbm, place_smem))
    others = [pltpu.make_async_copy(*ends, sems.at[slices + i]) for i, ends in enumerate(sources)]
    for move in whole + others:
        move.start()
    lower = iota((det, det), 1) < det // 2
    for s in range(slices):
        whole[s].wait()
        for parity, message_ref in zip(parities, message_refs):
            right = is_right(column, parity)
            real, imag = tile_ref[s, 0], tile_ref[s, 1]
            to_right = jnp.where(lower, half_roll(real), imag)
            to_left = jnp.where(lower, real, half_roll(imag))
            message_ref[s] = jnp.where(right, to_right, to_left)
    for move in others:
        move.wait()
    for dim in range(2):
        place_ref[dim] = jnp.full(place_ref.shape[1:], place_smem[dim], jnp.int32)


def corner_kernel(parities, row_axis, *refs):
    count = len(parities)
    message_refs, corner_refs = refs[:count], refs[count + 2 :]
    det = message_refs[0].shape[1]
    row_parity = lax.rem(lax.axis_index(row_axis), 2)
    for edge, corner_ref in enumerate(corner_refs):
        first = half_rows(det, row_parity, edge)
        for j, message_ref in enumerate(message_refs):
            corner_ref[j] = message_ref[:, pl.ds(first, det // 2)]


class Window:
    def __init__(self, parities, row_axis, column_axis, place_ref, tile_ref, *refs):
        count = len(parities)
        self.tile, self.edges, self.corners, self.messages = tile_ref, refs[:2], refs[2:4], refs[4 : 4 + count]
        self.even_row = lax.rem(lax.axis_index(row_axis), 2) == 0
        self.on_edge = [has_partner(row_axis, parity) for parity in range(2)]
        column = lax.axis_index(column_axis)
        self.across = [(has_partner(column_axis, parity), is_right(column, parity)) for parity in parities]
        self.row, self.col = scalar(place_ref, 0), scalar(place_ref, 1)

    def rows_of(self, pair_refs, index, middle):
        even, odd = [jnp.where(there, ref[index], 0.0) for there, ref in zip(self.on_edge, pair_refs)]
        above, below = jnp.where(self.even_row, odd, even), jnp.where(self.even_row, even, odd)
        return window_rows(above, middle, below, self.row)

    def store(self, s, window_ref):
        det = self.tile.shape[-1]
        lanes = iota((det, det), 1)
        lower, late = lanes < det // 2, lanes >= self.col
        messages = [self.rows_of(self.corners, (j, s), ref[s]) for j, ref in enumerate(self.messages)]
        for c in range(2):
            own = half_roll(self.rows_of(self.edges, (s, c), self.tile[s, c]))
            left, right = jnp.zeros_like(own), jnp.zeros_like(own)
            for (there, at_right), message in zip(self.across, messages):
                turned = half_roll(message)
                right = right + jnp.where(there & at_right, turned if c == 0 else message, 0.0)
                left = left + jnp.where(there & ~at_right, message if c == 0 else turned, 0.0)
            mixed = jnp.where(late, jnp.where(lower, left, own), jnp.where(lower, own, right))
            window = pltpu.roll(mixed, lax.rem(det - self.col, det), 1)
            window_ref[s, c] = window.T if s % 2 == 1 else window


def first_forward_kernel(parities, row_axis, column_axis, table_ref, probe_ref, *refs):
    window_ref, state_refs = refs[-4], refs[-3:]
    window = Window(parities, row_axis, column_axis, *refs[:-4])
    run_forward(window_ref, table_ref, [probe_ref], [], *state_refs, prepare=window.store)


def forward_kernel(probe_count, window_ref, table_ref, *refs):
    run_forward(window_ref, table_ref, refs[:probe_count], refs[probe_count:-3], *refs[-3:])


def run_forward(window_ref, table_ref, probe_refs, before_refs, wave_ref, far_ref, intensity_ref, prepare=None):
    slices, _, det, _ = window_ref.shape
    slots = [ref.at[j] for ref in probe_refs for j in range(ref.shape[0])]
    total = jnp.zeros((det, det), F32)
    for s in range(slices):
        if prepare is not None:
            prepare(s, window_ref)
        real, imag = window_ref[s, 0], window_ref[s, 1]
        last = s == slices - 1
        for mode, probe in enumerate(slots):
            source = probe if s == 0 else wave_ref.at[s - 1, mode]
            wave_real, wave_imag = source[0], source[1]
            leave_real = wave_real * real - wave_imag * imag
            leave_imag = wave_real * imag + wave_imag * real
            out_real, out_imag = two_sided(leave_real, leave_imag, table_ref, FOURIER if last else MOVE)
            target = far_ref.at[mode] if last else wave_ref.at[s, mode]
            target[0] = out_real
            target[1] = out_imag
            if last:
                total = total + (out_real * out_real + out_imag * out_imag)
    for before_ref in before_refs:
        total = total + before_ref[...]
    intensity_ref[...] = total


def backward_kernel(parities, parts, mode_axis, column_axis, place_ref, *refs):
    count = len(parities)
    measured_ref, mine_ref, other_ref, table_ref, window_ref = refs[count : count + 5]
    refs = refs[count + 5 :]
    probe_refs, refs = refs[: sum(parts)], refs[sum(parts) :]
    wave_refs, far_refs, refs = refs[: len(parts)], refs[len(parts) : 2 * len(parts)], refs[2 * len(parts) :]
    center_ref, send_ref = refs[:2]
    strip_refs, send_strip_refs = refs[2 : 2 + count], refs[2 + count : 2 + 2 * count]
    term_ref, back_ref = refs[2 + 2 * count :]
    slices, _, det, _ = window_ref.shape
    col = scalar(place_ref, 1)
    me = lax.axis_index(mode_axis)
    peer = me + 1 - 2 * lax.rem(me, 2)
    column = lax.axis_index(column_axis)
    probes = [ref.at[j] for ref in probe_refs for j in range(ref.shape[0])]
    slots = [(k, j) for k, ref in enumerate(far_refs) for j in range(ref.shape[0])]
    intensity = mine_ref[...] + other_ref[...]
    weight = 1.0 - measured_ref[...] / jnp.maximum(jnp.sqrt(intensity), 1.0)
    for s in reversed(range(slices)):
        last = s == slices - 1
        now, before = s % 2, (s + 1) % 2
        if not last:
            real, imag = window_ref[s + 1, 0], window_ref[s + 1, 1]
        for mode, (k, j) in enumerate(slots):
            if last:
                pulled_real, pulled_imag = weight * far_refs[k][j, 0], weight * far_refs[k][j, 1]
            else:
                back_real, back_imag = back_ref[before, mode, 0], back_ref[before, mode, 1]
                pulled_real = real * back_real + imag * back_imag
                pulled_imag = real * back_imag - imag * back_real
            base = FOURIER_BACK if last else MOVE_BACK
            back_real, back_imag = two_sided(pulled_real, pulled_imag, table_ref, base)
            back_ref[now, mode, 0] = back_real
            back_ref[now, mode, 1] = back_imag
        for first in range(0, det, ROWS):
            rows = slice(first, first + ROWS)
            term_real, term_imag = jnp.zeros((ROWS, det), F32), jnp.zeros((ROWS, det), F32)
            for mode, (k, j) in enumerate(slots):
                wave = wave_refs[k].at[s - 1, j] if s > 0 else probes[mode]
                wave_real, wave_imag = wave[0, rows], wave[1, rows]
                back_real, back_imag = back_ref[now, mode, 0, rows], back_ref[now, mode, 1, rows]
                term_real = term_real + (wave_real * back_real + wave_imag * back_imag)
                term_imag = term_imag + (wave_real * back_imag - wave_imag * back_real)
            term_ref[s, 0, rows] = term_real
            term_ref[s, 1, rows] = term_imag
        if s % 2 == 1:
            for c in range(2):
                term_ref[s, c] = term_ref[s, c].T

    lanes = iota((det, det), 1)
    lower, late = lanes < det // 2, lanes >= col
    forth_shift = lax.rem(col, det)
    for owner, middle_ref, out_strip_refs in ((me, center_ref, strip_refs), (peer, send_ref, send_strip_refs)):
        early, latter = [], []
        for c in range(2):
            turned = pltpu.roll(term_ref[owner, c], forth_shift, 1)
            early.append(jnp.where(late, turned, 0.0))
            latter.append(jnp.where(late, 0.0, turned))
            middle_ref[c] = half_roll(jnp.where(lower, latter[c], early[c]))
        to_right = jnp.where(lower, half_roll(latter[0]), latter[1])
        to_left = jnp.where(lower, early[0], half_roll(early[1]))
        for parity, strip_ref in zip(parities, out_strip_refs):
            strip_ref[...] = jnp.where(is_right(column, parity), to_right, to_left)


def place_kernel(parities, row_axis, column_axis, place_ref, mine_ref, other_ref, *refs):
    count = len(parities)
    place_refs, one_refs, two_refs = refs[:count], refs[count : 2 * count], refs[2 * count : 3 * count]
    middle_ref, even_ref, odd_ref = refs[3 * count :]
    even_row = lax.rem(lax.axis_index(row_axis), 2) == 0
    det = mine_ref.shape[1]
    half = det // 2
    column = lax.axis_index(column_axis)
    rows, lower = iota((det, det), 0), iota((det, det), 1) < half
    start = scalar(place_ref, 0)

    def placed(plane, begin):
        turned = pltpu.roll(plane, lax.rem(begin, det), 0)
        late = rows >= begin
        return jnp.where(late, turned, 0.0), jnp.where(late, 0.0, turned)

    blocks = [list(placed(mine_ref[c] + other_ref[c], start)) for c in range(2)]
    for parity, partner_ref, one_ref, two_ref in zip(parities, place_refs, one_refs, two_refs):
        strip = jnp.where(has_partner(column_axis, parity), one_ref[...] + two_ref[...], 0.0)
        at_right = is_right(column, parity)
        for block, part in enumerate(placed(strip, scalar(partner_ref, 0))):
            turned = half_roll(part)
            real = jnp.where(lower != at_right, jnp.where(at_right, turned, part), 0.0)
            imag = jnp.where(lower != at_right, jnp.where(at_right, part, turned), 0.0)
            blocks[0][block] = blocks[0][block] + real
            blocks[1][block] = blocks[1][block] + imag
    for c in range(2):
        first, second = blocks[c]
        middle_ref[c, :half] = first[half:]
        middle_ref[c, half:] = second[:half]
        even_ref[c] = jnp.where(even_row, second[half:], first[:half])
        odd_ref[c] = jnp.where(even_row, first[:half], second[half:])


HBM_SPEC = pl.BlockSpec(memory_space=pltpu.HBM)
VMEM_SPEC = pl.BlockSpec(memory_space=pltpu.VMEM)


def call(kernel, outs, operands, scratch=(), in_spec=VMEM_SPEC):
    return pl.pallas_call(
        kernel,
        out_shape=outs,
        in_specs=[in_spec] * len(operands),
        out_specs=[VMEM_SPEC] * len(outs),
        scratch_shapes=scratch,
        compiler_params=pltpu.CompilerParams(vmem_limit_bytes=VMEM_LIMIT),
    )(*operands)


def body(object_slices, probe_modes, positions, measured):
    modes_here, _, det, _ = probe_modes.shape
    slices, half = object_slices.shape[0], det // 2
    groups, height, width = lax.axis_size("mode"), lax.axis_size("ty"), lax.axis_size("tx")

    def edges(size, parity):
        ends = [(i, (i + 1) % size) for i in range(parity, size, 2)]
        return ends + [(j, i) for i, j in ends]

    parities = (0,) if width == 2 else (0, 1)
    count = len(parities)
    mirror = [(i, groups - 1 - i) for i in range(groups)]
    neighbour = edges(groups, 0)

    def shape(*sizes):
        return jax.ShapeDtypeStruct(sizes, F32)

    place, tile, part, even, odd, *messages = call(
        functools.partial(start_kernel, parities, "ty", "tx"),
        [
            jax.ShapeDtypeStruct((2, 8, 128), jnp.int32),
            shape(*object_slices.shape),
            shape(modes_here // SHARES, 2, det, det),
            shape(slices, 2, half, det),
            shape(slices, 2, half, det),
        ]
        + [shape(slices, det, det)] * count,
        [pltpu.with_memory_space_constraint(x, pltpu.HBM) for x in (positions.reshape(2), object_slices, probe_modes)],
        scratch=[pltpu.SMEM((2,), jnp.int32), pltpu.SemaphoreType.DMA((slices + 4,))],
        in_spec=HBM_SPEC,
    )
    fetched = lax.ppermute(part, "mode", mirror)
    messages = [lax.ppermute(block, "tx", edges(width, parity)) for parity, block in zip(parities, messages)]
    borders = [lax.ppermute(block, "ty", edges(height, edge)) for edge, block in enumerate((even, odd))]
    corners = call(
        functools.partial(corner_kernel, parities, "ty"),
        [shape(count, slices, half, det)] * 2,
        [*messages, *borders],
    )
    corners = [lax.ppermute(block, "ty", edges(height, edge)) for edge, block in enumerate(corners)]
    fetched, *_ = lax.optimization_barrier((fetched, *corners))
    fetched = [fetched, lax.ppermute(fetched, "ty", edges(height, 0))]

    table = jnp.asarray(tables(det))

    def states(modes):
        return [shape(slices - 1, modes, 2, det, det), shape(modes, 2, det, det), shape(det, det)]

    window, wave, far, mine = call(
        functools.partial(first_forward_kernel, parities, "ty", "tx"),
        [shape(slices, 2, det, det)] + states(modes_here),
        [table, probe_modes, place, tile, *borders, *corners, *messages],
    )
    more_wave, more_far, mine = call(
        functools.partial(forward_kernel, SHARES), states(modes_here), [window, table, *fetched, mine]
    )
    other = lax.ppermute(mine, "mode", neighbour)
    place, _ = lax.optimization_barrier((place, mine))
    partner_places = [lax.ppermute(place, "tx", edges(width, parity)) for parity in parities]
    amplitudes = measured.reshape(det, det)
    center, send, *strips = call(
        functools.partial(backward_kernel, parities, (1, SHARES), "mode", "tx"),
        [shape(2, det, det)] * 2 + [shape(det, det)] * (2 * count),
        [place, *partner_places, amplitudes if slices % 2 == 0 else amplitudes.T, mine, other]
        + [table, window, probe_modes, *fetched, wave, more_wave, far, more_far],
        scratch=[pltpu.VMEM((slices, 2, det, det), F32), pltpu.VMEM((2, 2 * modes_here, 2, det, det), F32)],
    )
    received = lax.ppermute(send, "mode", neighbour)
    ones = [lax.ppermute(block, "tx", edges(width, parity)) for parity, block in zip(parities, strips[:count])]
    twos = []
    for parity, block in zip(parities, strips[count:]):
        route = [(i * width + p, j * width + q) for i, j in neighbour for p, q in edges(width, parity)]
        twos.append(lax.ppermute(block, ("mode", "tx"), route))
    middle, even, odd = call(
        functools.partial(place_kernel, parities, "ty", "tx"),
        [shape(2, det, det), shape(2, half, det), shape(2, half, det)],
        [place, center, received, *partner_places, *ones, *twos],
    )
    even, odd = [
        jnp.where(has_partner("ty", edge), lax.ppermute(block, "ty", edges(height, edge)), 0.0)
        for edge, block in enumerate((even, odd))
    ]
    even_row = lax.rem(lax.axis_index("ty"), 2) == 0
    border = jnp.concatenate([jnp.where(even_row, odd, even), jnp.where(even_row, even, odd)], 1)
    return (middle + border)[None]


def solution(mesh):
    return jax.shard_map(
        body,
        mesh=mesh,
        in_specs=(
            P(None, None, "ty", "tx"),
            P("mode", None, None, None),
            P("ty", "tx", None, None),
            P("ty", "tx", None, None, None),
        ),
        out_specs=P("mode", None, "ty", "tx"),
        check_vma=False,
    )
```

```python
import functools

import jax
import jax.numpy as jnp
import numpy as np
from jax import lax
from jax.experimental import pallas as pl
from jax.experimental.pallas import tpu as pltpu
from jax.sharding import PartitionSpec as P

FRESNEL_RATE = 0.3
F32, BF16 = jnp.float32, jnp.bfloat16
VMEM_LIMIT = 24 * 2**20
ROWS = 32
SHARES = 2
MOVE, MOVE_BACK, FOURIER, FOURIER_BACK = 0, 2, 4, 6


def pair(table):
    high = table.astype(jnp.bfloat16)
    return [high, (table - high.astype(np.float64)).astype(jnp.bfloat16)]


def tables(length):
    counter = np.arange(length)
    fourier = np.exp(-2j * np.pi / length * (np.outer(counter, counter) % length)) / np.sqrt(length)
    frequency = np.where(counter < length // 2, counter, counter - length).astype(np.float64)
    chirp = np.exp(-1j * FRESNEL_RATE * frequency**2 / length)
    moved = fourier.conj() @ (chirp[:, None] * fourier)
    stacked = []
    for matrix in (moved, fourier):
        right = np.block([[matrix.real, matrix.imag], [-matrix.imag, matrix.real]])
        stacked += pair(right) + pair(right.T)
    return np.stack(stacked)


def dot(left, right):
    return jnp.dot(left, right, preferred_element_type=F32)


def split(value):
    high = value.astype(BF16)
    return high, (value - high.astype(F32)).astype(BF16)


def one_side(real, imag, table_ref, base):
    high, low = split(jnp.concatenate([real, imag], 1))
    both = dot(high, table_ref[base]) + dot(low, table_ref[base]) + dot(high, table_ref[base + 1])
    det = real.shape[1]
    return both[:, :det], both[:, det:]


def two_sided(real, imag, table_ref, base):
    upper_real, upper_imag = one_side(real, imag, table_ref, base)
    return one_side(upper_real.T, upper_imag.T, table_ref, base)


def iota(shape, dim):
    return lax.broadcasted_iota(jnp.int32, shape, dim)


def half_roll(plane):
    return pltpu.roll(plane, plane.shape[1] // 2, 1)


def is_right(index, parity):
    return lax.rem(index, 2) == parity


def has_partner(axis, parity):
    index = lax.axis_index(axis)
    first = index - lax.rem(index + parity, 2)
    return (first >= 0) & (first + 1 < lax.axis_size(axis))


def scalar(ref, *index):
    return jnp.max(ref[index])


def window_rows(above, tile, below, start):
    det = tile.shape[0]
    half = det // 2
    first = jnp.concatenate([above, tile[:half]], 0)
    second = jnp.concatenate([tile[half:], below], 0)
    mixed = jnp.where(iota(first.shape, 0) >= start, first, second)
    return pltpu.roll(mixed, lax.rem(det - start, det), 0)


def half_rows(ref_slice, row_parity, edge):
    half = ref_slice // 2
    return pl.multiple_of(jnp.where(row_parity == edge, half, 0), half)


def start_kernel(parities, row_axis, column_axis, place_hbm, tile_hbm, probe_hbm, *refs):
    count = len(parities)
    place_ref, tile_ref, part_ref, refs = refs[0], refs[1], refs[2], refs[3:]
    edge_refs, message_refs, place_smem, sems = refs[:2], refs[2 : 2 + count], refs[2 + count], refs[3 + count]
    slices, _, det, _ = tile_ref.shape
    share = part_ref.shape[0]
    row = lax.axis_index(row_axis)
    row_parity = lax.rem(row, 2)
    column = lax.axis_index(column_axis)
    whole = [pltpu.make_async_copy(tile_hbm.at[s], tile_ref.at[s], sems.at[s]) for s in range(slices)]
    sources = [(probe_hbm.at[pl.ds(lax.rem(row, SHARES) * share, share)], part_ref)]
    for edge, edge_ref in enumerate(edge_refs):
        first = half_rows(det, row_parity, edge)
        sources.append((tile_hbm.at[:, :, pl.ds(first, det // 2)], edge_ref))
    sources.append((place_hbm, place_smem))
    others = [pltpu.make_async_copy(*ends, sems.at[slices + i]) for i, ends in enumerate(sources)]
    for move in whole + others:
        move.start()
    lower = iota((det, det), 1) < det // 2
    for s in range(slices):
        whole[s].wait()
        for parity, message_ref in zip(parities, message_refs):
            right = is_right(column, parity)
            real, imag = tile_ref[s, 0], tile_ref[s, 1]
            to_right = jnp.where(lower, half_roll(real), imag)
            to_left = jnp.where(lower, real, half_roll(imag))
            message_ref[s * det : (s + 1) * det] = jnp.where(right, to_right, to_left)
    for move in others:
        move.wait()
    for dim in range(2):
        place_ref[dim] = jnp.full(place_ref.shape[1:], place_smem[dim], jnp.int32)
    for message_ref in message_refs:
        message_ref[slices * det :] = place_ref[0].astype(F32)


def corner_kernel(parities, row_axis, *refs):
    count = len(parities)
    message_refs, corner_refs, place_refs = refs[:count], refs[count + 2 : count + 4], refs[count + 4 :]
    _, slices, half, det = corner_refs[0].shape
    row_parity = lax.rem(lax.axis_index(row_axis), 2)
    for j, (message_ref, place_ref) in enumerate(zip(message_refs, place_refs)):
        place_ref[...] = message_ref[slices * det :].astype(jnp.int32)
        for edge, corner_ref in enumerate(corner_refs):
            first = half_rows(det, row_parity, edge)
            for s in range(slices):
                corner_ref[j, s] = message_ref[pl.ds(s * det + first, half)]


class Window:
    def __init__(self, parities, row_axis, column_axis, place_ref, tile_ref, *refs):
        count = len(parities)
        self.tile, self.edges, self.corners, self.messages = tile_ref, refs[:2], refs[2:4], refs[4 : 4 + count]
        self.even_row = lax.rem(lax.axis_index(row_axis), 2) == 0
        self.on_edge = [has_partner(row_axis, parity) for parity in range(2)]
        column = lax.axis_index(column_axis)
        self.across = [(has_partner(column_axis, parity), is_right(column, parity)) for parity in parities]
        self.row, self.col = scalar(place_ref, 0), scalar(place_ref, 1)

    def rows_of(self, pair_refs, index, middle):
        even, odd = [jnp.where(there, ref[index], 0.0) for there, ref in zip(self.on_edge, pair_refs)]
        above, below = jnp.where(self.even_row, odd, even), jnp.where(self.even_row, even, odd)
        return window_rows(above, middle, below, self.row)

    def store(self, s, window_ref):
        det = self.tile.shape[-1]
        lanes = iota((det, det), 1)
        lower, late = lanes < det // 2, lanes >= self.col
        messages = [self.rows_of(self.corners, (j, s), ref[s * det : (s + 1) * det]) for j, ref in enumerate(self.messages)]
        for c in range(2):
            own = half_roll(self.rows_of(self.edges, (s, c), self.tile[s, c]))
            left, right = jnp.zeros_like(own), jnp.zeros_like(own)
            for (there, at_right), message in zip(self.across, messages):
                turned = half_roll(message)
                right = right + jnp.where(there & at_right, turned if c == 0 else message, 0.0)
                left = left + jnp.where(there & ~at_right, message if c == 0 else turned, 0.0)
            mixed = jnp.where(late, jnp.where(lower, left, own), jnp.where(lower, own, right))
            window = pltpu.roll(mixed, lax.rem(det - self.col, det), 1)
            window_ref[s, c] = window.T if s % 2 == 1 else window


def first_forward_kernel(parities, row_axis, column_axis, table_ref, probe_ref, *refs):
    window_ref, state_refs = refs[-4], refs[-3:]
    window = Window(parities, row_axis, column_axis, *refs[:-4])
    run_forward(window_ref, table_ref, [probe_ref], [], *state_refs, prepare=window.store)


def forward_kernel(probe_count, window_ref, table_ref, *refs):
    run_forward(window_ref, table_ref, refs[:probe_count], refs[probe_count:-3], *refs[-3:])


def run_forward(window_ref, table_ref, probe_refs, before_refs, wave_ref, far_ref, intensity_ref, prepare=None):
    slices, _, det, _ = window_ref.shape
    slots = [ref.at[j] for ref in probe_refs for j in range(ref.shape[0])]
    total = jnp.zeros((det, det), F32)
    for s in range(slices):
        if prepare is not None:
            prepare(s, window_ref)
        real, imag = window_ref[s, 0], window_ref[s, 1]
        last = s == slices - 1
        for mode, probe in enumerate(slots):
            source = probe if s == 0 else wave_ref.at[s - 1, mode]
            wave_real, wave_imag = source[0], source[1]
            leave_real = wave_real * real - wave_imag * imag
            leave_imag = wave_real * imag + wave_imag * real
            out_real, out_imag = two_sided(leave_real, leave_imag, table_ref, FOURIER if last else MOVE)
            target = far_ref.at[mode] if last else wave_ref.at[s, mode]
            target[0] = out_real
            target[1] = out_imag
            if last:
                total = total + (out_real * out_real + out_imag * out_imag)
    for before_ref in before_refs:
        total = total + before_ref[...]
    intensity_ref[...] = total


def backward_kernel(parities, parts, mode_axis, column_axis, place_ref, *refs):
    count = len(parities)
    measured_ref, mine_ref, other_ref, table_ref, window_ref = refs[count : count + 5]
    refs = refs[count + 5 :]
    probe_refs, refs = refs[: sum(parts)], refs[sum(parts) :]
    wave_refs, far_refs, refs = refs[: len(parts)], refs[len(parts) : 2 * len(parts)], refs[2 * len(parts) :]
    center_ref, send_ref = refs[:2]
    strip_refs, send_strip_refs = refs[2 : 2 + count], refs[2 + count : 2 + 2 * count]
    term_ref, back_ref = refs[2 + 2 * count :]
    slices, _, det, _ = window_ref.shape
    col = scalar(place_ref, 1)
    me = lax.axis_index(mode_axis)
    peer = me + 1 - 2 * lax.rem(me, 2)
    column = lax.axis_index(column_axis)
    probes = [ref.at[j] for ref in probe_refs for j in range(ref.shape[0])]
    slots = [(k, j) for k, ref in enumerate(far_refs) for j in range(ref.shape[0])]
    intensity = mine_ref[...] + other_ref[...]
    weight = 1.0 - measured_ref[...] / jnp.maximum(jnp.sqrt(intensity), 1.0)
    for s in reversed(range(slices)):
        last = s == slices - 1
        now, before = s % 2, (s + 1) % 2
        if not last:
            real, imag = window_ref[s + 1, 0], window_ref[s + 1, 1]
        for mode, (k, j) in enumerate(slots):
            if last:
                pulled_real, pulled_imag = weight * far_refs[k][j, 0], weight * far_refs[k][j, 1]
            else:
                back_real, back_imag = back_ref[before, mode, 0], back_ref[before, mode, 1]
                pulled_real = real * back_real + imag * back_imag
                pulled_imag = real * back_imag - imag * back_real
            base = FOURIER_BACK if last else MOVE_BACK
            back_real, back_imag = two_sided(pulled_real, pulled_imag, table_ref, base)
            back_ref[now, mode, 0] = back_real
            back_ref[now, mode, 1] = back_imag
        for first in range(0, det, ROWS):
            rows = slice(first, first + ROWS)
            term_real, term_imag = jnp.zeros((ROWS, det), F32), jnp.zeros((ROWS, det), F32)
            for mode, (k, j) in enumerate(slots):
                wave = wave_refs[k].at[s - 1, j] if s > 0 else probes[mode]
                wave_real, wave_imag = wave[0, rows], wave[1, rows]
                back_real, back_imag = back_ref[now, mode, 0, rows], back_ref[now, mode, 1, rows]
                term_real = term_real + (wave_real * back_real + wave_imag * back_imag)
                term_imag = term_imag + (wave_real * back_imag - wave_imag * back_real)
            term_ref[s, 0, rows] = term_real
            term_ref[s, 1, rows] = term_imag
        if s % 2 == 1:
            for c in range(2):
                term_ref[s, c] = term_ref[s, c].T

    lanes = iota((det, det), 1)
    lower, late = lanes < det // 2, lanes >= col
    forth_shift = lax.rem(col, det)
    for owner, middle_ref, out_strip_refs in ((me, center_ref, strip_refs), (peer, send_ref, send_strip_refs)):
        early, latter = [], []
        for c in range(2):
            turned = pltpu.roll(term_ref[owner, c], forth_shift, 1)
            early.append(jnp.where(late, turned, 0.0))
            latter.append(jnp.where(late, 0.0, turned))
            middle_ref[c] = half_roll(jnp.where(lower, latter[c], early[c]))
        to_right = jnp.where(lower, half_roll(latter[0]), latter[1])
        to_left = jnp.where(lower, early[0], half_roll(early[1]))
        for parity, strip_ref in zip(parities, out_strip_refs):
            strip_ref[...] = jnp.where(is_right(column, parity), to_right, to_left)


def place_kernel(parities, row_axis, column_axis, place_ref, mine_ref, other_ref, *refs):
    count = len(parities)
    place_refs, one_refs, two_refs = refs[:count], refs[count : 2 * count], refs[2 * count : 3 * count]
    middle_ref, even_ref, odd_ref = refs[3 * count :]
    even_row = lax.rem(lax.axis_index(row_axis), 2) == 0
    det = mine_ref.shape[1]
    half = det // 2
    column = lax.axis_index(column_axis)
    rows, lower = iota((det, det), 0), iota((det, det), 1) < half
    start = scalar(place_ref, 0)

    def placed(plane, begin):
        turned = pltpu.roll(plane, lax.rem(begin, det), 0)
        late = rows >= begin
        return jnp.where(late, turned, 0.0), jnp.where(late, 0.0, turned)

    blocks = [list(placed(mine_ref[c] + other_ref[c], start)) for c in range(2)]
    for parity, partner_ref, one_ref, two_ref in zip(parities, place_refs, one_refs, two_refs):
        strip = jnp.where(has_partner(column_axis, parity), one_ref[...] + two_ref[...], 0.0)
        at_right = is_right(column, parity)
        for block, part in enumerate(placed(strip, scalar(partner_ref))):
            turned = half_roll(part)
            real = jnp.where(lower != at_right, jnp.where(at_right, turned, part), 0.0)
            imag = jnp.where(lower != at_right, jnp.where(at_right, part, turned), 0.0)
            blocks[0][block] = blocks[0][block] + real
            blocks[1][block] = blocks[1][block] + imag
    for c in range(2):
        first, second = blocks[c]
        middle_ref[c, :half] = first[half:]
        middle_ref[c, half:] = second[:half]
        even_ref[c] = jnp.where(even_row, second[half:], first[:half])
        odd_ref[c] = jnp.where(even_row, first[:half], second[half:])


HBM_SPEC = pl.BlockSpec(memory_space=pltpu.HBM)
VMEM_SPEC = pl.BlockSpec(memory_space=pltpu.VMEM)


def call(kernel, outs, operands, scratch=(), in_spec=VMEM_SPEC):
    return pl.pallas_call(
        kernel,
        out_shape=outs,
        in_specs=[in_spec] * len(operands),
        out_specs=[VMEM_SPEC] * len(outs),
        scratch_shapes=scratch,
        compiler_params=pltpu.CompilerParams(vmem_limit_bytes=VMEM_LIMIT),
    )(*operands)


def body(object_slices, probe_modes, positions, measured):
    modes_here, _, det, _ = probe_modes.shape
    slices, half = object_slices.shape[0], det // 2
    groups, height, width = lax.axis_size("mode"), lax.axis_size("ty"), lax.axis_size("tx")

    def edges(size, parity):
        ends = [(i, (i + 1) % size) for i in range(parity, size, 2)]
        return ends + [(j, i) for i, j in ends]

    parities = (0,) if width == 2 else (0, 1)
    count = len(parities)
    mirror = [(i, groups - 1 - i) for i in range(groups)]
    neighbour = edges(groups, 0)

    def shape(*sizes):
        return jax.ShapeDtypeStruct(sizes, F32)

    place, tile, part, even, odd, *messages = call(
        functools.partial(start_kernel, parities, "ty", "tx"),
        [
            jax.ShapeDtypeStruct((2, 8, det), jnp.int32),
            shape(*object_slices.shape),
            shape(modes_here // SHARES, 2, det, det),
            shape(slices, 2, half, det),
            shape(slices, 2, half, det),
        ]
        + [shape(slices * det + 8, det)] * count,
        [pltpu.with_memory_space_constraint(x, pltpu.HBM) for x in (positions.reshape(2), object_slices, probe_modes)],
        scratch=[pltpu.SMEM((2,), jnp.int32), pltpu.SemaphoreType.DMA((slices + 4,))],
        in_spec=HBM_SPEC,
    )
    fetched = lax.ppermute(part, "mode", mirror)
    messages = [lax.ppermute(block, "tx", edges(width, parity)) for parity, block in zip(parities, messages)]
    borders = [lax.ppermute(block, "ty", edges(height, edge)) for edge, block in enumerate((even, odd))]
    packed = call(
        functools.partial(corner_kernel, parities, "ty"),
        [shape(count, slices, half, det)] * 2 + [jax.ShapeDtypeStruct((8, det), jnp.int32)] * count,
        [*messages, *borders],
    )
    corners, partner_places = packed[:2], packed[2:]
    corners = [lax.ppermute(block, "ty", edges(height, edge)) for edge, block in enumerate(corners)]
    fetched, *_ = lax.optimization_barrier((fetched, *corners))
    fetched = [fetched, lax.ppermute(fetched, "ty", edges(height, 0))]

    table = jnp.asarray(tables(det))

    def states(modes):
        return [shape(slices - 1, modes, 2, det, det), shape(modes, 2, det, det), shape(det, det)]

    window, wave, far, mine = call(
        functools.partial(first_forward_kernel, parities, "ty", "tx"),
        [shape(slices, 2, det, det)] + states(modes_here),
        [table, probe_modes, place, tile, *borders, *corners, *messages],
    )
    more_wave, more_far, mine = call(
        functools.partial(forward_kernel, SHARES), states(modes_here), [window, table, *fetched, mine]
    )
    other = lax.ppermute(mine, "mode", neighbour)
    amplitudes = measured.reshape(det, det)
    center, send, *strips = call(
        functools.partial(backward_kernel, parities, (1, SHARES), "mode", "tx"),
        [shape(2, det, det)] * 2 + [shape(det, det)] * (2 * count),
        [place, *partner_places, amplitudes if slices % 2 == 0 else amplitudes.T, mine, other]
        + [table, window, probe_modes, *fetched, wave, more_wave, far, more_far],
        scratch=[pltpu.VMEM((slices, 2, det, det), F32), pltpu.VMEM((2, 2 * modes_here, 2, det, det), F32)],
    )
    received = lax.ppermute(send, "mode", neighbour)
    ones = [lax.ppermute(block, "tx", edges(width, parity)) for parity, block in zip(parities, strips[:count])]
    twos = []
    for parity, block in zip(parities, strips[count:]):
        route = [(i * width + p, j * width + q) for i, j in neighbour for p, q in edges(width, parity)]
        twos.append(lax.ppermute(block, ("mode", "tx"), route))
    middle, even, odd = call(
        functools.partial(place_kernel, parities, "ty", "tx"),
        [shape(2, det, det), shape(2, half, det), shape(2, half, det)],
        [place, center, received, *partner_places, *ones, *twos],
    )
    even, odd = [
        jnp.where(has_partner("ty", edge), lax.ppermute(block, "ty", edges(height, edge)), 0.0)
        for edge, block in enumerate((even, odd))
    ]
    even_row = lax.rem(lax.axis_index("ty"), 2) == 0
    border = jnp.concatenate([jnp.where(even_row, odd, even), jnp.where(even_row, even, odd)], 1)
    return (middle + border)[None]


def solution(mesh):
    return jax.shard_map(
        body,
        mesh=mesh,
        in_specs=(
            P(None, None, "ty", "tx"),
            P("mode", None, None, None),
            P("ty", "tx", None, None),
            P("ty", "tx", None, None, None),
        ),
        out_specs=P("mode", None, "ty", "tx"),
        check_vma=False,
    )
```

```python
import functools

import jax
import jax.numpy as jnp
import numpy as np
from jax import lax
from jax.experimental import pallas as pl
from jax.experimental.pallas import tpu as pltpu
from jax.sharding import PartitionSpec as P

FRESNEL_RATE = 0.3
F32, BF16 = jnp.float32, jnp.bfloat16
VMEM_LIMIT = 24 * 2**20
SHARES = 2
MOVE, MOVE_BACK, FOURIER, FOURIER_BACK = 0, 2, 4, 6


def pair(table):
    high = table.astype(jnp.bfloat16)
    return [high, (table - high.astype(np.float64)).astype(jnp.bfloat16)]


def tables(length):
    counter = np.arange(length)
    fourier = np.exp(-2j * np.pi / length * (np.outer(counter, counter) % length)) / np.sqrt(length)
    frequency = np.where(counter < length // 2, counter, counter - length).astype(np.float64)
    chirp = np.exp(-1j * FRESNEL_RATE * frequency**2 / length)
    moved = fourier.conj() @ (chirp[:, None] * fourier)
    stacked = []
    for matrix in (moved, fourier):
        right = np.block([[matrix.real, matrix.imag], [-matrix.imag, matrix.real]])
        stacked += pair(right) + pair(right.T)
    return np.stack(stacked)


def dot(left, right):
    return jnp.dot(left, right, preferred_element_type=F32)


def split(value):
    high = value.astype(BF16)
    return high, (value - high.astype(F32)).astype(BF16)


def one_side(real, imag, table_ref, base):
    high, low = split(jnp.concatenate([real, imag], 1))
    rows, det = real.shape
    stacked = dot(jnp.concatenate([high, low], 0), table_ref[base])
    both = stacked[:rows] + stacked[rows:] + dot(high, table_ref[base + 1])
    return both[:, :det], both[:, det:]


def two_sided(real, imag, table_ref, base):
    upper_real, upper_imag = one_side(real, imag, table_ref, base)
    return one_side(upper_real.T, upper_imag.T, table_ref, base)


def iota(shape, dim):
    return lax.broadcasted_iota(jnp.int32, shape, dim)


def half_roll(plane):
    return pltpu.roll(plane, plane.shape[1] // 2, 1)


def is_right(index, parity):
    return lax.rem(index, 2) == parity


def has_partner(axis, parity):
    index = lax.axis_index(axis)
    first = index - lax.rem(index + parity, 2)
    return (first >= 0) & (first + 1 < lax.axis_size(axis))


def scalar(ref, *index):
    return jnp.max(ref[index])


def window_rows(above, tile, below, start):
    det = tile.shape[0]
    half = det // 2
    first = jnp.concatenate([above, tile[:half]], 0)
    second = jnp.concatenate([tile[half:], below], 0)
    mixed = jnp.where(iota(first.shape, 0) >= start, first, second)
    return pltpu.roll(mixed, lax.rem(det - start, det), 0)


def half_rows(ref_slice, row_parity, edge):
    half = ref_slice // 2
    return pl.multiple_of(jnp.where(row_parity == edge, half, 0), half)


def start_kernel(parities, row_axis, column_axis, place_hbm, tile_hbm, probe_hbm, *refs):
    count = len(parities)
    place_ref, tile_ref, part_ref, refs = refs[0], refs[1], refs[2], refs[3:]
    edge_refs, message_refs, place_smem, sems = refs[:2], refs[2 : 2 + count], refs[2 + count], refs[3 + count]
    slices, _, det, _ = tile_ref.shape
    share = part_ref.shape[0]
    row = lax.axis_index(row_axis)
    row_parity = lax.rem(row, 2)
    column = lax.axis_index(column_axis)
    whole = [pltpu.make_async_copy(tile_hbm.at[s], tile_ref.at[s], sems.at[s]) for s in range(slices)]
    sources = [(probe_hbm.at[pl.ds(lax.rem(row, SHARES) * share, share)], part_ref)]
    for edge, edge_ref in enumerate(edge_refs):
        first = half_rows(det, row_parity, edge)
        sources.append((tile_hbm.at[:, :, pl.ds(first, det // 2)], edge_ref))
    sources.append((place_hbm, place_smem))
    others = [pltpu.make_async_copy(*ends, sems.at[slices + i]) for i, ends in enumerate(sources)]
    for move in whole + others:
        move.start()
    lower = iota((det, det), 1) < det // 2
    for s in range(slices):
        whole[s].wait()
        for parity, message_ref in zip(parities, message_refs):
            right = is_right(column, parity)
            real, imag = tile_ref[s, 0], tile_ref[s, 1]
            to_right = jnp.where(lower, half_roll(real), imag)
            to_left = jnp.where(lower, real, half_roll(imag))
            message_ref[s] = jnp.where(right, to_right, to_left)
    for move in others:
        move.wait()
    for dim in range(2):
        place_ref[dim] = jnp.full(place_ref.shape[1:], place_smem[dim], jnp.int32)


def corner_kernel(parities, row_axis, *refs):
    count = len(parities)
    message_refs, corner_refs = refs[:count], refs[count + 2 :]
    det = message_refs[0].shape[1]
    row_parity = lax.rem(lax.axis_index(row_axis), 2)
    for edge, corner_ref in enumerate(corner_refs):
        first = half_rows(det, row_parity, edge)
        for j, message_ref in enumerate(message_refs):
            corner_ref[j] = message_ref[:, pl.ds(first, det // 2)]


class Window:
    def __init__(self, parities, row_axis, column_axis, place_ref, tile_ref, *refs):
        count = len(parities)
        self.tile, self.edges, self.corners, self.messages = tile_ref, refs[:2], refs[2:4], refs[4 : 4 + count]
        self.even_row = lax.rem(lax.axis_index(row_axis), 2) == 0
        self.on_edge = [has_partner(row_axis, parity) for parity in range(2)]
        column = lax.axis_index(column_axis)
        self.across = [(has_partner(column_axis, parity), is_right(column, parity)) for parity in parities]
        self.row, self.col = scalar(place_ref, 0), scalar(place_ref, 1)

    def rows_of(self, pair_refs, index, middle):
        even, odd = [jnp.where(there, ref[index], 0.0) for there, ref in zip(self.on_edge, pair_refs)]
        above, below = jnp.where(self.even_row, odd, even), jnp.where(self.even_row, even, odd)
        return window_rows(above, middle, below, self.row)

    def store(self, s, window_ref):
        det = self.tile.shape[-1]
        lanes = iota((det, det), 1)
        lower, late = lanes < det // 2, lanes >= self.col
        messages = [self.rows_of(self.corners, (j, s), ref[s]) for j, ref in enumerate(self.messages)]
        for c in range(2):
            own = half_roll(self.rows_of(self.edges, (s, c), self.tile[s, c]))
            left, right = jnp.zeros_like(own), jnp.zeros_like(own)
            for (there, at_right), message in zip(self.across, messages):
                turned = half_roll(message)
                right = right + jnp.where(there & at_right, turned if c == 0 else message, 0.0)
                left = left + jnp.where(there & ~at_right, message if c == 0 else turned, 0.0)
            mixed = jnp.where(late, jnp.where(lower, left, own), jnp.where(lower, own, right))
            window = pltpu.roll(mixed, lax.rem(det - self.col, det), 1)
            window_ref[s, c] = window.T if s % 2 == 1 else window


def first_forward_kernel(parities, row_axis, column_axis, table_ref, probe_ref, *refs):
    window_ref, state_refs = refs[-4], refs[-3:]
    window = Window(parities, row_axis, column_axis, *refs[:-4])
    run_forward(window_ref, table_ref, [probe_ref], [], *state_refs, prepare=window.store)


def forward_kernel(probe_count, window_ref, table_ref, *refs):
    run_forward(window_ref, table_ref, refs[:probe_count], refs[probe_count:-3], *refs[-3:])


def run_forward(window_ref, table_ref, probe_refs, before_refs, wave_ref, far_ref, intensity_ref, prepare=None):
    slices, _, det, _ = window_ref.shape
    slots = [ref.at[j] for ref in probe_refs for j in range(ref.shape[0])]
    total = jnp.zeros((det, det), F32)
    for s in range(slices):
        if prepare is not None:
            prepare(s, window_ref)
        real, imag = window_ref[s, 0], window_ref[s, 1]
        last = s == slices - 1
        for mode, probe in enumerate(slots):
            source = probe if s == 0 else wave_ref.at[s - 1, mode]
            wave_real, wave_imag = source[0], source[1]
            leave_real = wave_real * real - wave_imag * imag
            leave_imag = wave_real * imag + wave_imag * real
            out_real, out_imag = two_sided(leave_real, leave_imag, table_ref, FOURIER if last else MOVE)
            target = far_ref.at[mode] if last else wave_ref.at[s, mode]
            target[0] = out_real
            target[1] = out_imag
            if last:
                total = total + (out_real * out_real + out_imag * out_imag)
    for before_ref in before_refs:
        total = total + before_ref[...]
    intensity_ref[...] = total


def backward_kernel(parities, parts, mode_axis, column_axis, place_ref, *refs):
    count = len(parities)
    measured_ref, mine_ref, other_ref, table_ref, window_ref = refs[count : count + 5]
    refs = refs[count + 5 :]
    probe_refs, refs = refs[: sum(parts)], refs[sum(parts) :]
    wave_refs, far_refs, refs = refs[: len(parts)], refs[len(parts) : 2 * len(parts)], refs[2 * len(parts) :]
    center_ref, send_ref = refs[:2]
    strip_refs, send_strip_refs = refs[2 : 2 + count], refs[2 + count : 2 + 2 * count]
    term_ref, back_ref = refs[2 + 2 * count :]
    slices, _, det, _ = window_ref.shape
    col = scalar(place_ref, 1)
    me = lax.axis_index(mode_axis)
    peer = me + 1 - 2 * lax.rem(me, 2)
    column = lax.axis_index(column_axis)
    probes = [ref.at[j] for ref in probe_refs for j in range(ref.shape[0])]
    slots = [(k, j) for k, ref in enumerate(far_refs) for j in range(ref.shape[0])]
    intensity = mine_ref[...] + other_ref[...]
    weight = 1.0 - measured_ref[...] / jnp.maximum(jnp.sqrt(intensity), 1.0)
    for s in reversed(range(slices)):
        last = s == slices - 1
        now, before = s % 2, (s + 1) % 2
        if not last:
            real, imag = window_ref[s + 1, 0], window_ref[s + 1, 1]
        for mode, (k, j) in enumerate(slots):
            if last:
                pulled_real, pulled_imag = weight * far_refs[k][j, 0], weight * far_refs[k][j, 1]
            else:
                back_real, back_imag = back_ref[before, mode, 0], back_ref[before, mode, 1]
                pulled_real = real * back_real + imag * back_imag
                pulled_imag = real * back_imag - imag * back_real
            base = FOURIER_BACK if last else MOVE_BACK
            back_real, back_imag = two_sided(pulled_real, pulled_imag, table_ref, base)
            back_ref[now, mode, 0] = back_real
            back_ref[now, mode, 1] = back_imag
            wave = wave_refs[k].at[s - 1, j] if s > 0 else probes[mode]
            term_real = wave[0] * back_real + wave[1] * back_imag
            term_imag = wave[0] * back_imag - wave[1] * back_real
            term_ref[s, 0] = term_real if mode == 0 else term_ref[s, 0] + term_real
            term_ref[s, 1] = term_imag if mode == 0 else term_ref[s, 1] + term_imag
        if s % 2 == 1:
            for c in range(2):
                term_ref[s, c] = term_ref[s, c].T

    lanes = iota((det, det), 1)
    lower, late = lanes < det // 2, lanes >= col
    forth_shift = lax.rem(col, det)
    for owner, middle_ref, out_strip_refs in ((me, center_ref, strip_refs), (peer, send_ref, send_strip_refs)):
        early, latter = [], []
        for c in range(2):
            turned = pltpu.roll(term_ref[owner, c], forth_shift, 1)
            early.append(jnp.where(late, turned, 0.0))
            latter.append(jnp.where(late, 0.0, turned))
            middle_ref[c] = half_roll(jnp.where(lower, latter[c], early[c]))
        to_right = jnp.where(lower, half_roll(latter[0]), latter[1])
        to_left = jnp.where(lower, early[0], half_roll(early[1]))
        for parity, strip_ref in zip(parities, out_strip_refs):
            strip_ref[...] = jnp.where(is_right(column, parity), to_right, to_left)


def place_kernel(parities, row_axis, column_axis, place_ref, mine_ref, other_ref, *refs):
    count = len(parities)
    place_refs, one_refs, two_refs = refs[:count], refs[count : 2 * count], refs[2 * count : 3 * count]
    middle_ref, even_ref, odd_ref = refs[3 * count :]
    even_row = lax.rem(lax.axis_index(row_axis), 2) == 0
    det = mine_ref.shape[1]
    half = det // 2
    column = lax.axis_index(column_axis)
    rows, lower = iota((det, det), 0), iota((det, det), 1) < half
    start = scalar(place_ref, 0)

    def placed(plane, begin):
        turned = pltpu.roll(plane, lax.rem(begin, det), 0)
        late = rows >= begin
        return jnp.where(late, turned, 0.0), jnp.where(late, 0.0, turned)

    blocks = [list(placed(mine_ref[c] + other_ref[c], start)) for c in range(2)]
    for parity, partner_ref, one_ref, two_ref in zip(parities, place_refs, one_refs, two_refs):
        strip = jnp.where(has_partner(column_axis, parity), one_ref[...] + two_ref[...], 0.0)
        at_right = is_right(column, parity)
        for block, part in enumerate(placed(strip, scalar(partner_ref, 0))):
            turned = half_roll(part)
            real = jnp.where(lower != at_right, jnp.where(at_right, turned, part), 0.0)
            imag = jnp.where(lower != at_right, jnp.where(at_right, part, turned), 0.0)
            blocks[0][block] = blocks[0][block] + real
            blocks[1][block] = blocks[1][block] + imag
    for c in range(2):
        first, second = blocks[c]
        middle_ref[c, :half] = first[half:]
        middle_ref[c, half:] = second[:half]
        even_ref[c] = jnp.where(even_row, second[half:], first[:half])
        odd_ref[c] = jnp.where(even_row, first[:half], second[half:])


HBM_SPEC = pl.BlockSpec(memory_space=pltpu.HBM)
VMEM_SPEC = pl.BlockSpec(memory_space=pltpu.VMEM)


def call(kernel, outs, operands, scratch=(), in_spec=VMEM_SPEC):
    return pl.pallas_call(
        kernel,
        out_shape=outs,
        in_specs=[in_spec] * len(operands),
        out_specs=[VMEM_SPEC] * len(outs),
        scratch_shapes=scratch,
        compiler_params=pltpu.CompilerParams(vmem_limit_bytes=VMEM_LIMIT),
    )(*operands)


def body(object_slices, probe_modes, positions, measured):
    modes_here, _, det, _ = probe_modes.shape
    slices, half = object_slices.shape[0], det // 2
    groups, height, width = lax.axis_size("mode"), lax.axis_size("ty"), lax.axis_size("tx")

    def edges(size, parity):
        ends = [(i, (i + 1) % size) for i in range(parity, size, 2)]
        return ends + [(j, i) for i, j in ends]

    parities = (0,) if width == 2 else (0, 1)
    count = len(parities)
    mirror = [(i, groups - 1 - i) for i in range(groups)]
    neighbour = edges(groups, 0)

    def shape(*sizes):
        return jax.ShapeDtypeStruct(sizes, F32)

    place, tile, part, even, odd, *messages = call(
        functools.partial(start_kernel, parities, "ty", "tx"),
        [
            jax.ShapeDtypeStruct((2, 8, 128), jnp.int32),
            shape(*object_slices.shape),
            shape(modes_here // SHARES, 2, det, det),
            shape(slices, 2, half, det),
            shape(slices, 2, half, det),
        ]
        + [shape(slices, det, det)] * count,
        [pltpu.with_memory_space_constraint(x, pltpu.HBM) for x in (positions.reshape(2), object_slices, probe_modes)],
        scratch=[pltpu.SMEM((2,), jnp.int32), pltpu.SemaphoreType.DMA((slices + 4,))],
        in_spec=HBM_SPEC,
    )
    fetched = lax.ppermute(part, "mode", mirror)
    messages = [lax.ppermute(block, "tx", edges(width, parity)) for parity, block in zip(parities, messages)]
    borders = [lax.ppermute(block, "ty", edges(height, edge)) for edge, block in enumerate((even, odd))]
    corners = call(
        functools.partial(corner_kernel, parities, "ty"),
        [shape(count, slices, half, det)] * 2,
        [*messages, *borders],
    )
    corners = [lax.ppermute(block, "ty", edges(height, edge)) for edge, block in enumerate(corners)]
    fetched, *_ = lax.optimization_barrier((fetched, *corners))
    fetched = [fetched, lax.ppermute(fetched, "ty", edges(height, 0))]

    table = jnp.asarray(tables(det))

    def states(modes):
        return [shape(slices - 1, modes, 2, det, det), shape(modes, 2, det, det), shape(det, det)]

    window, wave, far, mine = call(
        functools.partial(first_forward_kernel, parities, "ty", "tx"),
        [shape(slices, 2, det, det)] + states(modes_here),
        [table, probe_modes, place, tile, *borders, *corners, *messages],
    )
    more_wave, more_far, mine = call(
        functools.partial(forward_kernel, SHARES), states(modes_here), [window, table, *fetched, mine]
    )
    other = lax.ppermute(mine, "mode", neighbour)
    place, _ = lax.optimization_barrier((place, mine))
    partner_places = [lax.ppermute(place, "tx", edges(width, parity)) for parity in parities]
    amplitudes = measured.reshape(det, det)
    center, send, *strips = call(
        functools.partial(backward_kernel, parities, (1, SHARES), "mode", "tx"),
        [shape(2, det, det)] * 2 + [shape(det, det)] * (2 * count),
        [place, *partner_places, amplitudes if slices % 2 == 0 else amplitudes.T, mine, other]
        + [table, window, probe_modes, *fetched, wave, more_wave, far, more_far],
        scratch=[pltpu.VMEM((slices, 2, det, det), F32), pltpu.VMEM((2, 2 * modes_here, 2, det, det), F32)],
    )
    received = lax.ppermute(send, "mode", neighbour)
    ones = [lax.ppermute(block, "tx", edges(width, parity)) for parity, block in zip(parities, strips[:count])]
    twos = []
    for parity, block in zip(parities, strips[count:]):
        route = [(i * width + p, j * width + q) for i, j in neighbour for p, q in edges(width, parity)]
        twos.append(lax.ppermute(block, ("mode", "tx"), route))
    middle, even, odd = call(
        functools.partial(place_kernel, parities, "ty", "tx"),
        [shape(2, det, det), shape(2, half, det), shape(2, half, det)],
        [place, center, received, *partner_places, *ones, *twos],
    )
    even, odd = [
        jnp.where(has_partner("ty", edge), lax.ppermute(block, "ty", edges(height, edge)), 0.0)
        for edge, block in enumerate((even, odd))
    ]
    even_row = lax.rem(lax.axis_index("ty"), 2) == 0
    border = jnp.concatenate([jnp.where(even_row, odd, even), jnp.where(even_row, even, odd)], 1)
    return (middle + border)[None]


def solution(mesh):
    return jax.shard_map(
        body,
        mesh=mesh,
        in_specs=(
            P(None, None, "ty", "tx"),
            P("mode", None, None, None),
            P("ty", "tx", None, None),
            P("ty", "tx", None, None, None),
        ),
        out_specs=P("mode", None, "ty", "tx"),
        check_vma=False,
    )
```

```python
import functools

import jax
import jax.numpy as jnp
import numpy as np
from jax import lax
from jax.experimental import pallas as pl
from jax.experimental.pallas import tpu as pltpu
from jax.sharding import PartitionSpec as P

FRESNEL_RATE = 0.3
F32, BF16 = jnp.float32, jnp.bfloat16
VMEM_LIMIT = 24 * 2**20
SHARES = 2
MOVE, MOVE_BACK, FOURIER, FOURIER_BACK = 0, 2, 4, 6


def pair(table):
    high = table.astype(jnp.bfloat16)
    return [high, (table - high.astype(np.float64)).astype(jnp.bfloat16)]


def tables(length):
    counter = np.arange(length)
    fourier = np.exp(-2j * np.pi / length * (np.outer(counter, counter) % length)) / np.sqrt(length)
    frequency = np.where(counter < length // 2, counter, counter - length).astype(np.float64)
    chirp = np.exp(-1j * FRESNEL_RATE * frequency**2 / length)
    moved = fourier.conj() @ (chirp[:, None] * fourier)
    stacked = []
    for matrix in (moved, fourier):
        right = np.block([[matrix.real, matrix.imag], [-matrix.imag, matrix.real]])
        stacked += pair(right) + pair(right.T)
    return np.stack(stacked)


def dot(left, right):
    return jnp.dot(left, right, preferred_element_type=F32)


def split(value):
    high = value.astype(BF16)
    return high, (value - high.astype(F32)).astype(BF16)


def one_side(real, imag, table_ref, base):
    high, low = split(jnp.concatenate([real, imag], 1))
    rows, det = real.shape
    stacked = dot(jnp.concatenate([high, low], 0), table_ref[base])
    both = stacked[:rows] + stacked[rows:] + dot(high, table_ref[base + 1])
    return both[:, :det], both[:, det:]


def two_sided(real, imag, table_ref, base):
    upper_real, upper_imag = one_side(real, imag, table_ref, base)
    return one_side(upper_real.T, upper_imag.T, table_ref, base)


def iota(shape, dim):
    return lax.broadcasted_iota(jnp.int32, shape, dim)


def half_roll(plane):
    return pltpu.roll(plane, plane.shape[1] // 2, 1)


def is_right(index, parity):
    return lax.rem(index, 2) == parity


def has_partner(axis, parity):
    index = lax.axis_index(axis)
    first = index - lax.rem(index + parity, 2)
    return (first >= 0) & (first + 1 < lax.axis_size(axis))


def scalar(ref, *index):
    return jnp.max(ref[index])


def window_rows(above, tile, below, start):
    det = tile.shape[0]
    half = det // 2
    first = jnp.concatenate([above, tile[:half]], 0)
    second = jnp.concatenate([tile[half:], below], 0)
    mixed = jnp.where(iota(first.shape, 0) >= start, first, second)
    return pltpu.roll(mixed, lax.rem(det - start, det), 0)


def half_rows(ref_slice, row_parity, edge):
    half = ref_slice // 2
    return pl.multiple_of(jnp.where(row_parity == edge, half, 0), half)


def start_kernel(parities, row_axis, column_axis, place_hbm, tile_hbm, probe_hbm, *refs):
    count = len(parities)
    place_ref, tile_ref, part_ref, refs = refs[0], refs[1], refs[2], refs[3:]
    edge_refs, message_refs, place_smem, sems = refs[:2], refs[2 : 2 + count], refs[2 + count], refs[3 + count]
    slices, _, det, _ = tile_ref.shape
    share = part_ref.shape[0]
    row = lax.axis_index(row_axis)
    row_parity = lax.rem(row, 2)
    column = lax.axis_index(column_axis)
    whole = [pltpu.make_async_copy(tile_hbm.at[s], tile_ref.at[s], sems.at[s]) for s in range(slices)]
    sources = [(probe_hbm.at[pl.ds(lax.rem(row, SHARES) * share, share)], part_ref)]
    sources.append((place_hbm, place_smem))
    others = [pltpu.make_async_copy(*ends, sems.at[slices + i]) for i, ends in enumerate(sources)]
    for move in others + whole:
        move.start()
    lower = iota((det, det), 1) < det // 2
    firsts = [half_rows(det, row_parity, edge) for edge in range(2)]
    for s in range(slices):
        whole[s].wait()
        for first, edge_ref in zip(firsts, edge_refs):
            edge_ref[s] = tile_ref[s, :, pl.ds(first, det // 2)]
        for parity, message_ref in zip(parities, message_refs):
            right = is_right(column, parity)
            real, imag = tile_ref[s, 0], tile_ref[s, 1]
            to_right = jnp.where(lower, half_roll(real), imag)
            to_left = jnp.where(lower, real, half_roll(imag))
            message_ref[s] = jnp.where(right, to_right, to_left)
    for move in others:
        move.wait()
    for dim in range(2):
        place_ref[dim] = jnp.full(place_ref.shape[1:], place_smem[dim], jnp.int32)


def corner_kernel(parities, row_axis, *refs):
    count = len(parities)
    message_refs, corner_refs = refs[:count], refs[count + 2 :]
    det = message_refs[0].shape[1]
    row_parity = lax.rem(lax.axis_index(row_axis), 2)
    for edge, corner_ref in enumerate(corner_refs):
        first = half_rows(det, row_parity, edge)
        for j, message_ref in enumerate(message_refs):
            corner_ref[j] = message_ref[:, pl.ds(first, det // 2)]


class Window:
    def __init__(self, parities, row_axis, column_axis, place_ref, tile_ref, *refs):
        count = len(parities)
        self.tile, self.edges, self.corners, self.messages = tile_ref, refs[:2], refs[2:4], refs[4 : 4 + count]
        self.even_row = lax.rem(lax.axis_index(row_axis), 2) == 0
        self.on_edge = [has_partner(row_axis, parity) for parity in range(2)]
        column = lax.axis_index(column_axis)
        self.across = [(has_partner(column_axis, parity), is_right(column, parity)) for parity in parities]
        self.row, self.col = scalar(place_ref, 0), scalar(place_ref, 1)

    def rows_of(self, pair_refs, index, middle):
        even, odd = [jnp.where(there, ref[index], 0.0) for there, ref in zip(self.on_edge, pair_refs)]
        above, below = jnp.where(self.even_row, odd, even), jnp.where(self.even_row, even, odd)
        return window_rows(above, middle, below, self.row)

    def store(self, s, window_ref):
        det = self.tile.shape[-1]
        lanes = iota((det, det), 1)
        lower, late = lanes < det // 2, lanes >= self.col
        messages = [self.rows_of(self.corners, (j, s), ref[s]) for j, ref in enumerate(self.messages)]
        for c in range(2):
            own = half_roll(self.rows_of(self.edges, (s, c), self.tile[s, c]))
            left, right = jnp.zeros_like(own), jnp.zeros_like(own)
            for (there, at_right), message in zip(self.across, messages):
                turned = half_roll(message)
                right = right + jnp.where(there & at_right, turned if c == 0 else message, 0.0)
                left = left + jnp.where(there & ~at_right, message if c == 0 else turned, 0.0)
            mixed = jnp.where(late, jnp.where(lower, left, own), jnp.where(lower, own, right))
            window = pltpu.roll(mixed, lax.rem(det - self.col, det), 1)
            window_ref[s, c] = window.T if s % 2 == 1 else window


def first_forward_kernel(parities, row_axis, column_axis, table_ref, probe_ref, *refs):
    window_ref, state_refs = refs[-4], refs[-3:]
    window = Window(parities, row_axis, column_axis, *refs[:-4])
    run_forward(window_ref, table_ref, [probe_ref], [], *state_refs, prepare=window.store)


def forward_kernel(probe_count, window_ref, table_ref, *refs):
    run_forward(window_ref, table_ref, refs[:probe_count], refs[probe_count:-3], *refs[-3:])


def run_forward(window_ref, table_ref, probe_refs, before_refs, wave_ref, far_ref, intensity_ref, prepare=None):
    slices, _, det, _ = window_ref.shape
    slots = [ref.at[j] for ref in probe_refs for j in range(ref.shape[0])]
    total = jnp.zeros((det, det), F32)
    for s in range(slices):
        if prepare is not None:
            prepare(s, window_ref)
        real, imag = window_ref[s, 0], window_ref[s, 1]
        last = s == slices - 1
        for mode, probe in enumerate(slots):
            source = probe if s == 0 else wave_ref.at[s - 1, mode]
            wave_real, wave_imag = source[0], source[1]
            leave_real = wave_real * real - wave_imag * imag
            leave_imag = wave_real * imag + wave_imag * real
            out_real, out_imag = two_sided(leave_real, leave_imag, table_ref, FOURIER if last else MOVE)
            target = far_ref.at[mode] if last else wave_ref.at[s, mode]
            target[0] = out_real
            target[1] = out_imag
            if last:
                total = total + (out_real * out_real + out_imag * out_imag)
    for before_ref in before_refs:
        total = total + before_ref[...]
    intensity_ref[...] = total


def backward_kernel(parities, parts, mode_axis, column_axis, place_ref, *refs):
    count = len(parities)
    measured_ref, mine_ref, other_ref, table_ref, window_ref = refs[count : count + 5]
    refs = refs[count + 5 :]
    probe_refs, refs = refs[: sum(parts)], refs[sum(parts) :]
    wave_refs, far_refs, refs = refs[: len(parts)], refs[len(parts) : 2 * len(parts)], refs[2 * len(parts) :]
    center_ref, send_ref = refs[:2]
    strip_refs, send_strip_refs = refs[2 : 2 + count], refs[2 + count : 2 + 2 * count]
    term_ref, back_ref = refs[2 + 2 * count :]
    slices, _, det, _ = window_ref.shape
    col = scalar(place_ref, 1)
    me = lax.axis_index(mode_axis)
    peer = me + 1 - 2 * lax.rem(me, 2)
    column = lax.axis_index(column_axis)
    probes = [ref.at[j] for ref in probe_refs for j in range(ref.shape[0])]
    slots = [(k, j) for k, ref in enumerate(far_refs) for j in range(ref.shape[0])]
    intensity = mine_ref[...] + other_ref[...]
    weight = 1.0 - measured_ref[...] / jnp.maximum(jnp.sqrt(intensity), 1.0)
    for s in reversed(range(slices)):
        last = s == slices - 1
        now, before = s % 2, (s + 1) % 2
        if not last:
            real, imag = window_ref[s + 1, 0], window_ref[s + 1, 1]
        for mode, (k, j) in enumerate(slots):
            if last:
                pulled_real, pulled_imag = weight * far_refs[k][j, 0], weight * far_refs[k][j, 1]
            else:
                back_real, back_imag = back_ref[before, mode, 0], back_ref[before, mode, 1]
                pulled_real = real * back_real + imag * back_imag
                pulled_imag = real * back_imag - imag * back_real
            base = FOURIER_BACK if last else MOVE_BACK
            back_real, back_imag = two_sided(pulled_real, pulled_imag, table_ref, base)
            back_ref[now, mode, 0] = back_real
            back_ref[now, mode, 1] = back_imag
            wave = wave_refs[k].at[s - 1, j] if s > 0 else probes[mode]
            term_real = wave[0] * back_real + wave[1] * back_imag
            term_imag = wave[0] * back_imag - wave[1] * back_real
            term_ref[s, 0] = term_real if mode == 0 else term_ref[s, 0] + term_real
            term_ref[s, 1] = term_imag if mode == 0 else term_ref[s, 1] + term_imag
        if s % 2 == 1:
            for c in range(2):
                term_ref[s, c] = term_ref[s, c].T

    lanes = iota((det, det), 1)
    lower, late = lanes < det // 2, lanes >= col
    forth_shift = lax.rem(col, det)
    for owner, middle_ref, out_strip_refs in ((me, center_ref, strip_refs), (peer, send_ref, send_strip_refs)):
        early, latter = [], []
        for c in range(2):
            turned = pltpu.roll(term_ref[owner, c], forth_shift, 1)
            early.append(jnp.where(late, turned, 0.0))
            latter.append(jnp.where(late, 0.0, turned))
            middle_ref[c] = half_roll(jnp.where(lower, latter[c], early[c]))
        to_right = jnp.where(lower, half_roll(latter[0]), latter[1])
        to_left = jnp.where(lower, early[0], half_roll(early[1]))
        for parity, strip_ref in zip(parities, out_strip_refs):
            strip_ref[...] = jnp.where(is_right(column, parity), to_right, to_left)


def place_kernel(parities, row_axis, column_axis, place_ref, mine_ref, other_ref, *refs):
    count = len(parities)
    place_refs, one_refs, two_refs = refs[:count], refs[count : 2 * count], refs[2 * count : 3 * count]
    middle_ref, even_ref, odd_ref = refs[3 * count :]
    even_row = lax.rem(lax.axis_index(row_axis), 2) == 0
    det = mine_ref.shape[1]
    half = det // 2
    column = lax.axis_index(column_axis)
    rows, lower = iota((det, det), 0), iota((det, det), 1) < half
    start = scalar(place_ref, 0)

    def placed(plane, begin):
        turned = pltpu.roll(plane, lax.rem(begin, det), 0)
        late = rows >= begin
        return jnp.where(late, turned, 0.0), jnp.where(late, 0.0, turned)

    blocks = [list(placed(mine_ref[c] + other_ref[c], start)) for c in range(2)]
    for parity, partner_ref, one_ref, two_ref in zip(parities, place_refs, one_refs, two_refs):
        strip = jnp.where(has_partner(column_axis, parity), one_ref[...] + two_ref[...], 0.0)
        at_right = is_right(column, parity)
        for block, part in enumerate(placed(strip, scalar(partner_ref, 0))):
            turned = half_roll(part)
            real = jnp.where(lower != at_right, jnp.where(at_right, turned, part), 0.0)
            imag = jnp.where(lower != at_right, jnp.where(at_right, part, turned), 0.0)
            blocks[0][block] = blocks[0][block] + real
            blocks[1][block] = blocks[1][block] + imag
    for c in range(2):
        first, second = blocks[c]
        middle_ref[c, :half] = first[half:]
        middle_ref[c, half:] = second[:half]
        even_ref[c] = jnp.where(even_row, second[half:], first[:half])
        odd_ref[c] = jnp.where(even_row, first[:half], second[half:])


HBM_SPEC = pl.BlockSpec(memory_space=pltpu.HBM)
VMEM_SPEC = pl.BlockSpec(memory_space=pltpu.VMEM)


def call(kernel, outs, operands, scratch=(), in_spec=VMEM_SPEC):
    return pl.pallas_call(
        kernel,
        out_shape=outs,
        in_specs=[in_spec] * len(operands),
        out_specs=[VMEM_SPEC] * len(outs),
        scratch_shapes=scratch,
        compiler_params=pltpu.CompilerParams(vmem_limit_bytes=VMEM_LIMIT),
    )(*operands)


def body(object_slices, probe_modes, positions, measured):
    modes_here, _, det, _ = probe_modes.shape
    slices, half = object_slices.shape[0], det // 2
    groups, height, width = lax.axis_size("mode"), lax.axis_size("ty"), lax.axis_size("tx")

    def edges(size, parity):
        ends = [(i, (i + 1) % size) for i in range(parity, size, 2)]
        return ends + [(j, i) for i, j in ends]

    parities = (0,) if width == 2 else (0, 1)
    count = len(parities)
    mirror = [(i, groups - 1 - i) for i in range(groups)]
    neighbour = edges(groups, 0)

    def shape(*sizes):
        return jax.ShapeDtypeStruct(sizes, F32)

    place, tile, part, even, odd, *messages = call(
        functools.partial(start_kernel, parities, "ty", "tx"),
        [
            jax.ShapeDtypeStruct((2, 8, 128), jnp.int32),
            shape(*object_slices.shape),
            shape(modes_here // SHARES, 2, det, det),
            shape(slices, 2, half, det),
            shape(slices, 2, half, det),
        ]
        + [shape(slices, det, det)] * count,
        [pltpu.with_memory_space_constraint(x, pltpu.HBM) for x in (positions.reshape(2), object_slices, probe_modes)],
        scratch=[pltpu.SMEM((2,), jnp.int32), pltpu.SemaphoreType.DMA((slices + 2,))],
        in_spec=HBM_SPEC,
    )
    fetched = lax.ppermute(part, "mode", mirror)
    messages = [lax.ppermute(block, "tx", edges(width, parity)) for parity, block in zip(parities, messages)]
    borders = [lax.ppermute(block, "ty", edges(height, edge)) for edge, block in enumerate((even, odd))]
    corners = call(
        functools.partial(corner_kernel, parities, "ty"),
        [shape(count, slices, half, det)] * 2,
        [*messages, *borders],
    )
    corners = [lax.ppermute(block, "ty", edges(height, edge)) for edge, block in enumerate(corners)]
    fetched, *_ = lax.optimization_barrier((fetched, *corners))
    fetched = [fetched, lax.ppermute(fetched, "ty", edges(height, 0))]

    table = jnp.asarray(tables(det))

    def states(modes):
        return [shape(slices - 1, modes, 2, det, det), shape(modes, 2, det, det), shape(det, det)]

    window, wave, far, mine = call(
        functools.partial(first_forward_kernel, parities, "ty", "tx"),
        [shape(slices, 2, det, det)] + states(modes_here),
        [table, probe_modes, place, tile, *borders, *corners, *messages],
    )
    more_wave, more_far, mine = call(
        functools.partial(forward_kernel, SHARES), states(modes_here), [window, table, *fetched, mine]
    )
    other = lax.ppermute(mine, "mode", neighbour)
    place, _ = lax.optimization_barrier((place, mine))
    partner_places = [lax.ppermute(place, "tx", edges(width, parity)) for parity in parities]
    amplitudes = measured.reshape(det, det)
    center, send, *strips = call(
        functools.partial(backward_kernel, parities, (1, SHARES), "mode", "tx"),
        [shape(2, det, det)] * 2 + [shape(det, det)] * (2 * count),
        [place, *partner_places, amplitudes if slices % 2 == 0 else amplitudes.T, mine, other]
        + [table, window, probe_modes, *fetched, wave, more_wave, far, more_far],
        scratch=[pltpu.VMEM((slices, 2, det, det), F32), pltpu.VMEM((2, 2 * modes_here, 2, det, det), F32)],
    )
    received = lax.ppermute(send, "mode", neighbour)
    ones = [lax.ppermute(block, "tx", edges(width, parity)) for parity, block in zip(parities, strips[:count])]
    twos = []
    for parity, block in zip(parities, strips[count:]):
        route = [(i * width + p, j * width + q) for i, j in neighbour for p, q in edges(width, parity)]
        twos.append(lax.ppermute(block, ("mode", "tx"), route))
    middle, even, odd = call(
        functools.partial(place_kernel, parities, "ty", "tx"),
        [shape(2, det, det), shape(2, half, det), shape(2, half, det)],
        [place, center, received, *partner_places, *ones, *twos],
    )
    even, odd = [
        jnp.where(has_partner("ty", edge), lax.ppermute(block, "ty", edges(height, edge)), 0.0)
        for edge, block in enumerate((even, odd))
    ]
    even_row = lax.rem(lax.axis_index("ty"), 2) == 0
    border = jnp.concatenate([jnp.where(even_row, odd, even), jnp.where(even_row, even, odd)], 1)
    return (middle + border)[None]


def solution(mesh):
    return jax.shard_map(
        body,
        mesh=mesh,
        in_specs=(
            P(None, None, "ty", "tx"),
            P("mode", None, None, None),
            P("ty", "tx", None, None),
            P("ty", "tx", None, None, None),
        ),
        out_specs=P("mode", None, "ty", "tx"),
        check_vma=False,
    )
```
